256 devices in a mesh: replica: 16 (over z_hi, y), fsdp: 16 (over z_lo, x, core).
Axes of the slice: x: 4, y: 4, z: 8 (z_hi: 4, z_lo: 2; z = z_hi * 2 + z_lo), core: 2. Of those that a mesh axis runs over, the one named last changes fastest.
Arguments:
- inner_weights: bfloat16 [16, 4, 1024, 8192], P('replica', None, 'fsdp'), may hold values from -6 to 6
- snapshot: bfloat16 [1024, 8192], P('fsdp'), may hold values from -6 to 6
- momentum: float32 [1024, 8192], P('fsdp', 'replica'), may hold values from -6 to 6
- rand_bits: int32 [16, 1024, 8192], P('replica', 'fsdp'), may hold values from 0 to 4095
- fragment: int32 [1], replicated, may hold values from 0 to 3
Outputs:
- new_snapshot: bfloat16 [1024, 8192], P('fsdp')
- new_momentum: float32 [1024, 8192], P('fsdp', 'replica')
- new_inner: bfloat16 [16, 4, 1024, 8192], P('replica', None, 'fsdp')
The draws below stay inside these ranges and needn't reach their ends.
Inputs may be any that keep to these rules, and one draw needn't show every extreme that they name: fragment[0] is one of 0, 1, 2, 3, the fragment of the window that syncs.
All inputs are finite; a program needn't handle non-finite values.
Results may differ from the reference program's by a relative error of at most 0.0075.
Values may be sent and summed in bfloat16 or wider, within the bound.
No kernel may reach another device: no remote copies, remote signals or barrier semaphores. Data moves between devices by JAX's collectives and lax.ppermute only.
A program may use at most 64 MiB of HBM per device.

```python
import jax
import jax.numpy as jnp
from jax import lax

D = 8192
KV = 1024
FRAGS = 4
REPLICAS = 16


def touch_ends(result, stream_key, smallest, high):
    longest = result.shape.index(max(result.shape))
    spots = []
    for shift in (0, 1):
        where = [jax.random.randint(jax.random.fold_in(stream_key, axis), (), 0, length) for axis, length in enumerate(result.shape)]
        where[longest] = (where[longest] + shift) % result.shape[longest]
        spots.append(tuple(where))
    return result.at[spots[0]].set(smallest).at[spots[1]].set(high)


def level_of(rng, dims, cuts, smallest, high):
    def one(position, parts):
        steps = jax.random.uniform(jax.random.fold_in(jax.random.fold_in(rng, 6), position), (parts,), jnp.float32, smallest / len(cuts), high / len(cuts))
        return jnp.repeat(jnp.exp(steps), dims[position] // parts).reshape((-1,) + (1,) * (len(dims) - position - 1))

    gain = one(*cuts[0])
    for cut in cuts[1:]:
        gain = gain * one(*cut)
    return gain


def gaussian(rng, extent, width, limit, split=(), kind=jnp.bfloat16):
    level = level_of(rng, extent, split, -0.22, 0.18) if split else 1.0
    result = jax.random.normal(rng, extent, jnp.float32) * width * level
    return jnp.minimum(jnp.maximum(result, -limit), limit).astype(kind)


def setup_inputs(seed: int = 0) -> dict:
    seeds = jax.random.split(jax.random.key(seed), 6)
    inner_weights = gaussian(seeds[0], (REPLICAS, FRAGS, KV, D), 1.0, 6.0, ((0, 16), (2, 16)))
    snapshot = gaussian(seeds[1], (KV, D), 1.0, 6.0, ((0, 16),))
    momentum = gaussian(seeds[2], (KV, D), 1.0, 6.0, ((0, 16), (1, 16)), jnp.float32)
    rand_bits = touch_ends(jax.random.randint(seeds[3], (REPLICAS, KV, D), 0, 4096), jax.random.fold_in(seeds[3], 1), 0, 4095).astype(jnp.int32)
    fragment = jax.random.randint(seeds[4], (1,), 0, FRAGS).astype(jnp.int32)
    return {"inner_weights": inner_weights, "snapshot": snapshot, "momentum": momentum, "rand_bits": rand_bits, "fragment": fragment}


momentum_coef = 0.9
outer_rate = 0.7
blend_keep = 0.5
grid_scale = 4.0
bit_levels = 4096.0


def stochastic_grid(snapshot, chosen, rand_bits):
    scaled = grid_scale * (snapshot.astype(jnp.float32) - chosen.astype(jnp.float32))
    lower = jnp.floor(scaled)
    raised = jnp.where(rand_bits.astype(jnp.float32) < bit_levels * (scaled - lower), 1.0, 0.0).astype(jnp.float32)
    return ((lower + raised) / grid_scale).astype(jnp.bfloat16)


def reference(inner_weights, snapshot, momentum, rand_bits, fragment):
    fragment_id = fragment[0].astype(jnp.int32)
    chosen_all = lax.dynamic_index_in_dim(inner_weights, fragment_id, 1, keepdims=False)

    def accumulate(summed, pair):
        chosen, bits = pair
        return summed + stochastic_grid(snapshot, chosen, bits).astype(jnp.float32), None

    summed, _ = lax.scan(accumulate, jnp.zeros(snapshot.shape, jnp.float32), (chosen_all, rand_bits))
    grad = summed / REPLICAS
    new_momentum = momentum_coef * momentum + grad
    new_snapshot = (snapshot.astype(jnp.float32) - outer_rate * (grad + momentum_coef * new_momentum)).astype(jnp.bfloat16)
    blended = (blend_keep * chosen_all.astype(jnp.float32) + (1.0 - blend_keep) * new_snapshot.astype(jnp.float32)[None]).astype(jnp.bfloat16)
    picked = lax.broadcasted_iota(jnp.int32, (1, FRAGS, 1, 1), 1) == fragment_id
    new_inner = jnp.where(picked, blended[:, None], inner_weights)
    return new_snapshot, new_momentum, new_inner
```

```python
import functools

import jax
import jax.numpy as jnp
from jax import lax
from jax.experimental import pallas as pl
from jax.experimental.pallas import tpu as pltpu
from jax.sharding import PartitionSpec as P

momentum_coef = 0.9
outer_rate = 0.7
blend_keep = 0.5
grid_scale = 4.0
bit_levels = 4096.0

Y = 4
Z = 4
CHUNKS = 2
ROWS = 32


def y_shift(k):
    return [(z * Y + y, z * Y + (y + k) % Y) for z in range(Z) for y in range(Y)]


def z_swap(s):
    return [(z * Y + y, (z ^ s) * Y + y) for z in range(Z) for y in range(Y)]


def round_kernel(share, ids, inner_ref, snap_ref, bits_ref, *outs):
    for k in range(Y):
        cols = pl.ds(pl.multiple_of(lax.rem(ids[1] + k, Y) * share, share), share)
        snap = snap_ref[:, cols].astype(jnp.float32)
        scaled = grid_scale * (snap - inner_ref[0, 0, :, cols].astype(jnp.float32))
        lower = jnp.floor(scaled)
        raised = jnp.where(
            bits_ref[0, :, cols].astype(jnp.float32) < bit_levels * (scaled - lower), 1.0, 0.0
        )
        centred = lower - jnp.floor(grid_scale * snap) + raised
        outs[k][...] = centred.astype(jnp.bfloat16)


def rounded_blocks(ids, inner, snapshot, bits, chunk, share):
    rows = snapshot.shape[0]
    wide = Y * share
    per = Z // CHUNKS
    first = chunk * per
    return pl.pallas_call(
        functools.partial(round_kernel, share),
        out_shape=[jax.ShapeDtypeStruct((rows, per * share), jnp.bfloat16)] * Y,
        grid_spec=pltpu.PrefetchScalarGridSpec(
            num_scalar_prefetch=1,
            grid=(per, rows // ROWS),
            in_specs=[
                pl.BlockSpec((1, 1, ROWS, wide), lambda j, i, ids: (0, ids[0], i, first + j)),
                pl.BlockSpec((ROWS, wide), lambda j, i, ids: (i, first + j)),
                pl.BlockSpec((1, ROWS, wide), lambda j, i, ids: (0, i, first + j)),
            ],
            out_specs=[pl.BlockSpec((ROWS, share), lambda j, i, ids: (i, j))] * Y,
        ),
        compiler_params=pltpu.CompilerParams(vmem_limit_bytes=8 << 20),
        cost_estimate=pl.CostEstimate(
            flops=12 * rows * per * wide, bytes_accessed=10 * rows * per * wide, transcendentals=0
        ),
        name=f"round{chunk}",
    )(ids, inner, snapshot, bits)


def copy_kernel(ids, inner_ref, out_ref, sems):
    frags = inner_ref.shape[1]
    copies = []
    for n in range(1, frags):
        f = lax.rem(ids[0] + n, frags)
        copies.append(pltpu.make_async_copy(inner_ref.at[0, f], out_ref.at[0, f], sems.at[n - 1]))
    for c in copies:
        c.start()
    for c in copies:
        c.wait()


def others_copied(ids, inner):
    frags = inner.shape[1]
    return pl.pallas_call(
        copy_kernel,
        out_shape=jax.ShapeDtypeStruct(inner.shape, inner.dtype),
        grid_spec=pltpu.PrefetchScalarGridSpec(
            num_scalar_prefetch=1,
            grid=(),
            in_specs=[pl.BlockSpec(memory_space=pl.ANY)],
            out_specs=pl.BlockSpec(memory_space=pl.ANY),
            scratch_shapes=[pltpu.SemaphoreType.DMA((frags - 1,))],
        ),
        compiler_params=pltpu.CompilerParams(vmem_limit_bytes=1 << 20),
        cost_estimate=pl.CostEstimate(flops=0, bytes_accessed=3 * inner.size, transcendentals=0),
        name="others",
    )(ids, inner)


def blend_kernel(share, ids, inner_ref, *refs):
    blocks, (snap_out, inner_out) = refs[:Y], refs[-2:]
    for k in range(Y):
        cols = pl.ds(pl.multiple_of(lax.rem(ids[1] + Y - k, Y) * share, share), share)
        new = blocks[k][...]
        snap_out[:, cols] = new
        inner_out[0, 0, :, cols] = (
            blend_keep * inner_ref[0, 0, :, cols].astype(jnp.float32)
            + (1.0 - blend_keep) * new.astype(jnp.float32)
        ).astype(jnp.bfloat16)


def blended(ids, inner, blocks, snap_out, inner_out, chunk, share):
    rows = blocks[0].shape[0]
    wide = Y * share
    per = Z // CHUNKS
    first = chunk * per
    inner_spec = pl.BlockSpec((1, 1, ROWS, wide), lambda j, i, ids: (0, ids[0], i, first + j))
    snap_spec = pl.BlockSpec((ROWS, wide), lambda j, i, ids: (i, first + j))
    kept = [inner_out] if snap_out is None else [snap_out, inner_out]
    last = 1 + 1 + Y + len(kept) - 1
    aliases = {last: 1} if snap_out is None else {last - 1: 0, last: 1}
    return pl.pallas_call(
        functools.partial(blend_kernel, share),
        out_shape=[
            jax.ShapeDtypeStruct((rows, Z * wide), jnp.bfloat16),
            jax.ShapeDtypeStruct(inner.shape, inner.dtype),
        ],
        grid_spec=pltpu.PrefetchScalarGridSpec(
            num_scalar_prefetch=1,
            grid=(per, rows // ROWS),
            in_specs=[inner_spec]
            + [pl.BlockSpec((ROWS, share), lambda j, i, ids: (i, j))] * Y
            + [pl.BlockSpec(memory_space=pl.ANY)] * len(kept),
            out_specs=[snap_spec, inner_spec],
        ),
        input_output_aliases=aliases,
        compiler_params=pltpu.CompilerParams(vmem_limit_bytes=8 << 20),
        cost_estimate=pl.CostEstimate(
            flops=4 * rows * per * wide, bytes_accessed=8 * rows * per * wide, transcendentals=0
        ),
        name=f"blend{chunk}",
    )(ids, inner, *blocks, *kept)


def body(inner, snapshot, momentum, bits, fragment):
    f32 = jnp.float32
    share = momentum.shape[1]
    me = lax.axis_index("replica")
    y, z = me % Y, me // Y
    ids = jnp.stack([fragment[0], y.astype(jnp.int32)])
    per = Z // CHUNKS

    near = lax.ppermute(momentum, "replica", z_swap(1))
    odd = z % 2 == 1
    mine = jnp.concatenate(
        [jnp.where(odd, near, momentum), jnp.where(odd, momentum, near)], axis=1
    )
    far = lax.ppermute(mine, "replica", z_swap(3))
    high = z // 2 == 1
    moments = jnp.concatenate([jnp.where(high, far, mine), jnp.where(high, mine, far)], axis=1)
    snaps = jnp.concatenate(
        [lax.dynamic_slice_in_dim(snapshot, (b * Y + y) * share, share, 1) for b in range(Z)], axis=1
    )

    sent = [rounded_blocks(ids, inner, snapshot, bits, c, share) for c in range(CHUNKS)]
    others = others_copied(ids, inner)
    totals, news = [], []
    for c in range(CHUNKS):
        got = [sent[c][0]] + [lax.ppermute(sent[c][k], "replica", y_shift(k)) for k in range(1, Y)]
        part = sum(g.astype(f32) for g in got).astype(jnp.bfloat16)
        order = (1, 3) if c % 2 == 0 else (3, 1)
        part = (
            part.astype(f32) + lax.ppermute(part, "replica", z_swap(order[0])).astype(f32)
        ).astype(jnp.bfloat16)
        total = part.astype(f32) + lax.ppermute(part, "replica", z_swap(order[1])).astype(f32)
        at = slice(c * per * share, (c + 1) * per * share)
        snap = snaps[:, at].astype(f32)
        grad = (total + (Y * Z) * jnp.floor(grid_scale * snap)) / (grid_scale * Y * Z)
        moment = momentum_coef * moments[:, at] + grad
        totals.append(grad)
        news.append((snap - outer_rate * (grad + momentum_coef * moment)).astype(jnp.bfloat16))

    snap_out, inner_out = None, others
    for c in range(CHUNKS):
        blocks = [news[c]] + [lax.ppermute(news[c], "replica", y_shift(k)) for k in range(1, Y)]
        snap_out, inner_out = blended(ids, inner, blocks, snap_out, inner_out, c, share)

    grads = jnp.concatenate(totals, axis=1)
    own = grads[:, :share]
    for b in range(1, Z):
        own = jnp.where(z == b, grads[:, b * share : (b + 1) * share], own)
    return snap_out, momentum_coef * momentum + own, inner_out


def solution(mesh):
    placed = (
        P("replica", None, "fsdp", None),
        P("fsdp", None),
        P("fsdp", "replica"),
        P("replica", "fsdp", None),
        P(),
    )
    return jax.shard_map(
        body,
        mesh=mesh,
        in_specs=placed,
        out_specs=(P("fsdp", None), P("fsdp", "replica"), P("replica", None, "fsdp", None)),
        check_vma=False,
    )
```

```python
import functools

import jax
import jax.numpy as jnp
from jax import lax
from jax.experimental import pallas as pl
from jax.experimental.pallas import tpu as pltpu
from jax.sharding import PartitionSpec as P

momentum_coef = 0.9
outer_rate = 0.7
blend_keep = 0.5
grid_scale = 4.0
bit_levels = 4096.0

Y = 4
Z = 4
CHUNKS = 2
PER = Z // CHUNKS
PIECES = 2


def y_shift(k):
    return [(z * Y + y, z * Y + (y + k) % Y) for z in range(Z) for y in range(Y)]


def z_swap(s):
    return [(z * Y + y, (z ^ s) * Y + y) for z in range(Z) for y in range(Y)]


def pinned(x):
    return pltpu.with_memory_space_constraint(x, pltpu.HBM)


def round_kernel(chunk, share, ids, after_ref, inner_hbm, snap_hbm, bits_hbm, *refs):
    outs, snap_out, chosen = refs[:Y], refs[Y], refs[Y + 1]
    snaps, draws, sems = refs[Y + 2 :]
    rows = snaps.shape[0]
    wide = PER * Y * share
    strip = rows // PIECES
    cols = pl.ds(chunk * wide, wide)
    copies = []
    for p in range(PIECES):
        at = pl.ds(p * strip, strip)
        copies.append(
            [
                pltpu.make_async_copy(src, dst.at[at], sems.at[p, n])
                for n, (src, dst) in enumerate(
                    (
                        (bits_hbm.at[0, at, cols], draws),
                        (inner_hbm.at[0, ids[0], at, cols], chosen),
                        (snap_hbm.at[at, cols], snaps),
                    )
                )
            ]
        )
        for c in copies[-1]:
            c.start()
    for p in range(PIECES):
        for c in copies[p]:
            c.wait()
        for k in range(Y):
            owner = lax.rem(ids[1] + k, Y)
            for j in range(PER):
                for i in range(strip // 16):
                    at = pl.ds(p * strip + i * 16, 16)
                    block = pl.ds(pl.multiple_of((j * Y + owner) * share, share), share)
                    raw = snaps[at, block]
                    snap = grid_scale * raw.astype(jnp.float32)
                    kept = grid_scale * chosen[at, block].astype(jnp.float32)
                    level = draws[at, block].astype(jnp.float32) * (1.0 / bit_levels)
                    centred = jnp.ceil((snap - kept) - level) - jnp.floor(snap)
                    outs[k][at, j * share : (j + 1) * share] = centred.astype(jnp.bfloat16)
                    if k == 0:
                        snap_out[at, j * share : (j + 1) * share] = raw


def rounded_blocks(ids, after, inner, snapshot, bits, chunk, share):
    rows = snapshot.shape[0]
    wide = PER * Y * share
    return pl.pallas_call(
        functools.partial(round_kernel, chunk, share),
        out_shape=[pltpu.VMEM((rows, PER * share), jnp.bfloat16)] * (Y + 1)
        + [pltpu.VMEM((rows, wide), jnp.bfloat16)],
        in_specs=[pl.BlockSpec(memory_space=pltpu.SMEM)]
        + [pl.BlockSpec(memory_space=pl.ANY)]
        + [pl.BlockSpec(memory_space=pltpu.HBM)] * 3,
        out_specs=[pl.BlockSpec(memory_space=pltpu.VMEM)] * (Y + 2),
        scratch_shapes=[
            pltpu.VMEM((rows, wide), jnp.bfloat16),
            pltpu.VMEM((rows, wide), jnp.int32),
            pltpu.SemaphoreType.DMA((PIECES, 3)),
        ],
        compiler_params=pltpu.CompilerParams(vmem_limit_bytes=12 << 20),
        cost_estimate=pl.CostEstimate(
            flops=12 * rows * wide, bytes_accessed=10 * rows * wide, transcendentals=0
        ),
        name=f"round{chunk}",
    )(ids, after, pinned(inner), pinned(snapshot), pinned(bits))


def copy_kernel(ids, after_ref, inner_hbm, out_hbm, held, sems):
    frags = inner_hbm.shape[1]
    rows = inner_hbm.shape[2]
    strip = rows // PIECES
    steps = []
    for n in range(1, frags):
        f = lax.rem(ids[0] + n, frags)
        for p in range(PIECES):
            at = pl.ds(p * strip, strip)
            slot = held.at[n - 1, at]
            steps.append(
                (
                    pltpu.make_async_copy(inner_hbm.at[0, f, at], slot, sems.at[n - 1, p, 0]),
                    pltpu.make_async_copy(slot, out_hbm.at[0, f, at], sems.at[n - 1, p, 1]),
                )
            )
    for load, _ in steps:
        load.start()
    for load, store in steps:
        load.wait()
        store.start()
    for _, store in steps:
        store.wait()


def others_copied(ids, after, inner):
    frags = inner.shape[1]
    return pl.pallas_call(
        copy_kernel,
        out_shape=jax.ShapeDtypeStruct(inner.shape, inner.dtype),
        in_specs=[
            pl.BlockSpec(memory_space=pltpu.SMEM),
            pl.BlockSpec(memory_space=pl.ANY),
            pl.BlockSpec(memory_space=pltpu.HBM),
        ],
        out_specs=pl.BlockSpec(memory_space=pltpu.HBM),
        scratch_shapes=[
            pltpu.VMEM((frags - 1, *inner.shape[2:]), inner.dtype),
            pltpu.SemaphoreType.DMA((frags - 1, PIECES, 2)),
        ],
        compiler_params=pltpu.CompilerParams(vmem_limit_bytes=12 << 20),
        cost_estimate=pl.CostEstimate(flops=0, bytes_accessed=3 * inner.size, transcendentals=0),
        name="others",
    )(ids, after, pinned(inner))


def blend_kernel(chunk, share, ids, chosen, *refs):
    blocks = refs[:Y]
    snap_hbm, inner_out, snaps, mixed, sems = refs[-5:]
    rows = snaps.shape[0]
    wide = PER * Y * share
    strip = rows // PIECES
    cols = pl.ds(chunk * wide, wide)
    copies = []
    for p in range(PIECES):
        for k in range(Y):
            owner = lax.rem(ids[1] + Y - k, Y)
            for j in range(PER):
                for i in range(strip // 16):
                    at = pl.ds(p * strip + i * 16, 16)
                    block = pl.ds(pl.multiple_of((j * Y + owner) * share, share), share)
                    new = blocks[k][at, j * share : (j + 1) * share]
                    snaps[at, block] = new
                    mixed[at, block] = (
                        blend_keep * chosen[at, block].astype(jnp.float32)
                        + (1.0 - blend_keep) * new.astype(jnp.float32)
                    ).astype(jnp.bfloat16)
        at = pl.ds(p * strip, strip)
        copies += [
            pltpu.make_async_copy(snaps.at[at], snap_hbm.at[at, cols], sems.at[p, 0]),
            pltpu.make_async_copy(mixed.at[at], inner_out.at[0, ids[0], at, cols], sems.at[p, 1]),
        ]
        for c in copies[-2:]:
            c.start()
    for c in copies:
        c.wait()


def blended(ids, chosen, blocks, snap_out, inner_out, chunk, share):
    rows = blocks[0].shape[0]
    wide = PER * Y * share
    kept = [inner_out] if snap_out is None else [snap_out, inner_out]
    last = 1 + 1 + Y + len(kept) - 1
    aliases = {last: 1} if snap_out is None else {last - 1: 0, last: 1}
    hbm = pl.BlockSpec(memory_space=pltpu.HBM)
    return pl.pallas_call(
        functools.partial(blend_kernel, chunk, share),
        out_shape=[
            jax.ShapeDtypeStruct((rows, CHUNKS * wide), jnp.bfloat16),
            jax.ShapeDtypeStruct(inner_out.shape, inner_out.dtype),
        ],
        in_specs=[pl.BlockSpec(memory_space=pltpu.SMEM)]
        + [pl.BlockSpec(memory_space=pltpu.VMEM)] * (Y + 1)
        + [hbm] * len(kept),
        out_specs=[hbm, hbm],
        scratch_shapes=[pltpu.VMEM((rows, wide), jnp.bfloat16)] * 2
        + [pltpu.SemaphoreType.DMA((PIECES, 2))],
        input_output_aliases=aliases,
        compiler_params=pltpu.CompilerParams(vmem_limit_bytes=12 << 20),
        cost_estimate=pl.CostEstimate(
            flops=4 * rows * wide, bytes_accessed=8 * rows * wide, transcendentals=0
        ),
        name=f"blend{chunk}",
    )(ids, chosen, *blocks, *kept)


def body(inner, snapshot, momentum, bits, fragment):
    f32, bf16 = jnp.float32, jnp.bfloat16
    share = momentum.shape[1]
    me = lax.axis_index("replica")
    y, z = lax.rem(me, Y), lax.div(me, Y)
    ids = jnp.stack([fragment[0], y.astype(jnp.int32)])

    def send(x, perm):
        return lax.ppermute(x, "replica", perm)

    near = send(momentum, z_swap(1))
    odd = lax.rem(z, 2) == 1
    mine = [jnp.where(odd, near, momentum), jnp.where(odd, momentum, near)]
    both = jnp.concatenate(mine, axis=1)
    far = send(both, z_swap(3))
    far = [far[:, :share], far[:, share:]]
    high = lax.div(z, 2) == 1
    moments = [jnp.where(high, b, a) for a, b in zip(mine, far)]
    moments += [jnp.where(high, a, b) for a, b in zip(mine, far)]

    sent, parts, snaps, kept = [], [], [], []
    for c in range(CHUNKS):
        *blocks, snap, chosen = rounded_blocks(
            ids, ids if c == 0 else both, inner, snapshot, bits, c, share
        )
        sent.append(blocks)
        snaps.append(snap)
        kept.append(chosen)
    for c in range(CHUNKS):
        got = [sent[c][0]] + [send(sent[c][k], y_shift(k)) for k in range(1, Y)]
        parts.append(sum(g.astype(f32) for g in got).astype(bf16))
    others = others_copied(ids, moments[0], inner)
    grads, news = [], []
    for c in range(CHUNKS):
        order = (1, 3) if c % 2 == 0 else (3, 1)
        part = parts[c]
        part = (part.astype(f32) + send(part, z_swap(order[0])).astype(f32)).astype(bf16)
        if c == CHUNKS - 1:
            part, others = lax.optimization_barrier((part, others))
        total = part.astype(f32) + send(part, z_swap(order[1])).astype(f32)
        snap = snaps[c].astype(f32)
        grad = (total + (Y * Z) * jnp.floor(grid_scale * snap)) / (grid_scale * Y * Z)
        gathered = jnp.concatenate([moments[c * PER + j] for j in range(PER)], axis=1)
        moment = momentum_coef * gathered + grad
        grads.append(grad)
        news.append((snap - outer_rate * (grad + momentum_coef * moment)).astype(bf16))

    snap_out, inner_out = None, others
    for c in range(CHUNKS):
        blocks = [news[c]] + [send(news[c], y_shift(k)) for k in range(1, Y)]
        snap_out, inner_out = blended(ids, kept[c], blocks, snap_out, inner_out, c, share)

    own = grads[0][:, :share]
    for b in range(1, Z):
        at = (b % PER) * share
        own = jnp.where(z == b, grads[b // PER][:, at : at + share], own)
    return snap_out, momentum_coef * momentum + own, inner_out


def solution(mesh):
    placed = (
        P("replica", None, "fsdp", None),
        P("fsdp", None),
        P("fsdp", "replica"),
        P("replica", "fsdp", None),
        P(),
    )
    return jax.shard_map(
        body,
        mesh=mesh,
        in_specs=placed,
        out_specs=(P("fsdp", None), P("fsdp", "replica"), P("replica", None, "fsdp", None)),
        check_vma=False,
    )
```

```python
import functools

import jax
import jax.numpy as jnp
from jax import lax
from jax.experimental import pallas as pl
from jax.experimental.pallas import tpu as pltpu
from jax.sharding import PartitionSpec as P

momentum_coef = 0.9
outer_rate = 0.7
blend_keep = 0.5
grid_scale = 4.0
bit_levels = 4096.0

Y = 4
Z = 4
CHUNKS = 2
PER = Z // CHUNKS
PIECES = 2
ORDER = (0, 3, 1, 2)


def y_shift(k):
    return [(z * Y + y, z * Y + (y + k) % Y) for z in range(Z) for y in range(Y)]


def z_swap(s):
    return [(z * Y + y, (z ^ s) * Y + y) for z in range(Z) for y in range(Y)]


def here():
    return lax.rem(lax.axis_index("replica"), Y)


def pinned(x):
    return pltpu.with_memory_space_constraint(x, pltpu.HBM)


def round_kernel(chunk, share, ids, after_ref, inner_hbm, snap_hbm, bits_hbm, *refs):
    outs, snap_out, chosen = refs[:Y], refs[Y], refs[Y + 1]
    snaps, draws, sems = refs[Y + 2 :]
    rows = snaps.shape[0]
    wide = PER * Y * share
    strip = rows // PIECES
    cols = pl.ds(chunk * wide, wide)
    copies = []
    for p in range(PIECES):
        at = pl.ds(p * strip, strip)
        copies.append(
            [
                pltpu.make_async_copy(src, dst.at[at], sems.at[p, n])
                for n, (src, dst) in enumerate(
                    (
                        (bits_hbm.at[0, at, cols], draws),
                        (inner_hbm.at[0, ids[0], at, cols], chosen),
                        (snap_hbm.at[at, cols], snaps),
                    )
                )
            ]
        )
        for c in copies[-1]:
            c.start()
    for p in range(PIECES):
        for c in copies[p]:
            c.wait()
        for k in range(Y):
            owner = lax.rem(here() + k, Y)
            for j in range(PER):
                for i in range(strip // 16):
                    at = pl.ds(p * strip + i * 16, 16)
                    block = pl.ds(pl.multiple_of((j * Y + owner) * share, share), share)
                    raw = snaps[at, block]
                    snap = grid_scale * raw.astype(jnp.float32)
                    kept = grid_scale * chosen[at, block].astype(jnp.float32)
                    level = draws[at, block].astype(jnp.float32) * (1.0 / bit_levels)
                    centred = jnp.ceil((snap - kept) - level) - jnp.floor(snap)
                    outs[k][at, j * share : (j + 1) * share] = centred.astype(jnp.bfloat16)
                    if k == 0:
                        snap_out[at, j * share : (j + 1) * share] = raw


def rounded_blocks(ids, after, inner, snapshot, bits, chunk, share):
    rows = snapshot.shape[0]
    wide = PER * Y * share
    return pl.pallas_call(
        functools.partial(round_kernel, chunk, share),
        out_shape=[pltpu.VMEM((rows, PER * share), jnp.bfloat16)] * (Y + 1)
        + [pltpu.VMEM((rows, wide), jnp.bfloat16)],
        in_specs=[pl.BlockSpec(memory_space=pltpu.SMEM)]
        + [pl.BlockSpec(memory_space=pl.ANY)]
        + [pl.BlockSpec(memory_space=pltpu.HBM)] * 3,
        out_specs=[pl.BlockSpec(memory_space=pltpu.VMEM)] * (Y + 2),
        scratch_shapes=[
            pltpu.VMEM((rows, wide), jnp.bfloat16),
            pltpu.VMEM((rows, wide), jnp.int32),
            pltpu.SemaphoreType.DMA((PIECES, 3)),
        ],
        compiler_params=pltpu.CompilerParams(vmem_limit_bytes=12 << 20),
        cost_estimate=pl.CostEstimate(
            flops=12 * rows * wide, bytes_accessed=10 * rows * wide, transcendentals=0
        ),
        name=f"round{chunk}",
    )(ids, after, pinned(inner), pinned(snapshot), pinned(bits))


def copy_kernel(ids, after_ref, inner_hbm, out_hbm, held, sems):
    frags = inner_hbm.shape[1]
    rows = inner_hbm.shape[2]
    strip = rows // PIECES
    steps = []
    for n in range(1, frags):
        f = lax.rem(ids[0] + n, frags)
        for p in range(PIECES):
            at = pl.ds(p * strip, strip)
            slot = held.at[n - 1, at]
            steps.append(
                (
                    pltpu.make_async_copy(inner_hbm.at[0, f, at], slot, sems.at[n - 1, p, 0]),
                    pltpu.make_async_copy(slot, out_hbm.at[0, f, at], sems.at[n - 1, p, 1]),
                )
            )
    for load, _ in steps:
        load.start()
    for load, store in steps:
        load.wait()
        store.start()
    for _, store in steps:
        store.wait()


def others_copied(ids, after, inner):
    frags = inner.shape[1]
    return pl.pallas_call(
        copy_kernel,
        out_shape=jax.ShapeDtypeStruct(inner.shape, inner.dtype),
        in_specs=[
            pl.BlockSpec(memory_space=pltpu.SMEM),
            pl.BlockSpec(memory_space=pl.ANY),
            pl.BlockSpec(memory_space=pltpu.HBM),
        ],
        out_specs=pl.BlockSpec(memory_space=pltpu.HBM),
        scratch_shapes=[
            pltpu.VMEM((frags - 1, *inner.shape[2:]), inner.dtype),
            pltpu.SemaphoreType.DMA((frags - 1, PIECES, 2)),
        ],
        compiler_params=pltpu.CompilerParams(vmem_limit_bytes=12 << 20),
        cost_estimate=pl.CostEstimate(flops=0, bytes_accessed=3 * inner.size, transcendentals=0),
        name="others",
    )(ids, after, pinned(inner))


def blend_kernel(chunk, share, ids, chosen, *refs):
    blocks = refs[:Y]
    snap_hbm, inner_out, snaps, mixed, sems = refs[-5:]
    rows = snaps.shape[0]
    wide = PER * Y * share
    strip = rows // PIECES
    cols = pl.ds(chunk * wide, wide)
    copies = []
    for p in range(PIECES):
        for n, k in enumerate(ORDER):
            owner = lax.rem(here() + Y - k, Y)
            for j in range(PER):
                for i in range(strip // 16):
                    at = pl.ds(p * strip + i * 16, 16)
                    block = pl.ds(pl.multiple_of((j * Y + owner) * share, share), share)
                    new = blocks[n][at, j * share : (j + 1) * share]
                    snaps[at, block] = new
                    mixed[at, block] = (
                        blend_keep * chosen[at, block].astype(jnp.float32)
                        + (1.0 - blend_keep) * new.astype(jnp.float32)
                    ).astype(jnp.bfloat16)
        at = pl.ds(p * strip, strip)
        copies += [
            pltpu.make_async_copy(snaps.at[at], snap_hbm.at[at, cols], sems.at[p, 0]),
            pltpu.make_async_copy(mixed.at[at], inner_out.at[0, ids[0], at, cols], sems.at[p, 1]),
        ]
        for c in copies[-2:]:
            c.start()
    for c in copies:
        c.wait()


def blended(ids, chosen, blocks, snap_out, inner_out, chunk, share):
    rows = blocks[0].shape[0]
    wide = PER * Y * share
    kept = [inner_out] if snap_out is None else [snap_out, inner_out]
    last = 1 + 1 + Y + len(kept) - 1
    aliases = {last: 1} if snap_out is None else {last - 1: 0, last: 1}
    hbm = pl.BlockSpec(memory_space=pltpu.HBM)
    return pl.pallas_call(
        functools.partial(blend_kernel, chunk, share),
        out_shape=[
            jax.ShapeDtypeStruct((rows, CHUNKS * wide), jnp.bfloat16),
            jax.ShapeDtypeStruct(inner_out.shape, inner_out.dtype),
        ],
        in_specs=[pl.BlockSpec(memory_space=pltpu.SMEM)]
        + [pl.BlockSpec(memory_space=pltpu.VMEM)] * (Y + 1)
        + [hbm] * len(kept),
        out_specs=[hbm, hbm],
        scratch_shapes=[pltpu.VMEM((rows, wide), jnp.bfloat16)] * 2
        + [pltpu.SemaphoreType.DMA((PIECES, 2))],
        input_output_aliases=aliases,
        compiler_params=pltpu.CompilerParams(vmem_limit_bytes=12 << 20),
        cost_estimate=pl.CostEstimate(
            flops=4 * rows * wide, bytes_accessed=8 * rows * wide, transcendentals=0
        ),
        name=f"blend{chunk}",
    )(ids, chosen, *blocks, *kept)


def body(inner, snapshot, momentum, bits, fragment):
    f32, bf16 = jnp.float32, jnp.bfloat16
    share = momentum.shape[1]
    me = lax.axis_index("replica")
    y, z = lax.rem(me, Y), lax.div(me, Y)
    ids = fragment

    def send(x, perm):
        return lax.ppermute(x, "replica", perm)

    near = send(momentum, z_swap(1))
    odd = lax.rem(z, 2) == 1
    mine = [jnp.where(odd, near, momentum), jnp.where(odd, momentum, near)]
    both = jnp.concatenate(mine, axis=1)
    far = send(both, z_swap(3))
    far = [far[:, :share], far[:, share:]]
    high = lax.div(z, 2) == 1
    moments = [jnp.where(high, b, a) for a, b in zip(mine, far)]
    moments += [jnp.where(high, a, b) for a, b in zip(mine, far)]

    sent, parts, snaps, kept = [], [], [], []
    for c in range(CHUNKS):
        *blocks, snap, chosen = rounded_blocks(
            ids, ids if c == 0 else both, inner, snapshot, bits, c, share
        )
        sent.append(blocks)
        snaps.append(snap)
        kept.append(chosen)
    for c in range(CHUNKS):
        got = [sent[c][0]] + [send(sent[c][k], y_shift(k)) for k in (2, 1, 3)]
        parts.append(sum(g.astype(f32) for g in got).astype(bf16))
    others = others_copied(ids, moments[0], inner)
    grads, news = [], []
    for c in range(CHUNKS):
        order = (1, 3) if c % 2 == 0 else (3, 1)
        part = parts[c]
        part = (part.astype(f32) + send(part, z_swap(order[0])).astype(f32)).astype(bf16)
        if c == CHUNKS - 1:
            part, others = lax.optimization_barrier((part, others))
        total = part.astype(f32) + send(part, z_swap(order[1])).astype(f32)
        snap = snaps[c].astype(f32)
        grad = (total + (Y * Z) * jnp.floor(grid_scale * snap)) / (grid_scale * Y * Z)
        gathered = jnp.concatenate([moments[c * PER + j] for j in range(PER)], axis=1)
        moment = momentum_coef * gathered + grad
        grads.append(grad)
        news.append((snap - outer_rate * (grad + momentum_coef * moment)).astype(bf16))

    snap_out, inner_out = None, others
    for c in range(CHUNKS):
        blocks = [news[c]] + [send(news[c], y_shift(k)) for k in ORDER[1:]]
        snap_out, inner_out = blended(ids, kept[c], blocks, snap_out, inner_out, c, share)

    own = grads[0][:, :share]
    for b in range(1, Z):
        at = (b % PER) * share
        own = jnp.where(z == b, grads[b // PER][:, at : at + share], own)
    return snap_out, momentum_coef * momentum + own, inner_out


def solution(mesh):
    placed = (
        P("replica", None, "fsdp", None),
        P("fsdp", None),
        P("fsdp", "replica"),
        P("replica", "fsdp", None),
        P(),
    )
    return jax.shard_map(
        body,
        mesh=mesh,
        in_specs=placed,
        out_specs=(P("fsdp", None), P("fsdp", "replica"), P("replica", None, "fsdp", None)),
        check_vma=False,
    )
```

```python
import functools

import jax
import jax.numpy as jnp
from jax import lax
from jax.experimental import pallas as pl
from jax.experimental.pallas import tpu as pltpu
from jax.sharding import PartitionSpec as P

momentum_coef = 0.9
outer_rate = 0.7
blend_keep = 0.5
grid_scale = 4.0
bit_levels = 4096.0

Y = 4
Z = 4
CHUNKS = 2
PER = Z // CHUNKS
PIECES = 2
ORDER = (0, 3, 1, 2)


def y_shift(k):
    return [(z * Y + y, z * Y + (y + k) % Y) for z in range(Z) for y in range(Y)]


def z_swap(s):
    return [(z * Y + y, (z ^ s) * Y + y) for z in range(Z) for y in range(Y)]


def here():
    return lax.rem(lax.axis_index("replica"), Y)


def pinned(x):
    return pltpu.with_memory_space_constraint(x, pltpu.HBM)


def round_kernel(chunk, share, ids, after_ref, inner_hbm, snap_hbm, bits_hbm, *refs):
    outs, snap_out, chosen = refs[:Y], refs[Y], refs[Y + 1]
    snaps, draws, sems = refs[Y + 2 :]
    rows = snaps.shape[0]
    wide = PER * Y * share
    strip = rows // PIECES
    cols = pl.ds(chunk * wide, wide)
    copies = []
    for p in range(PIECES):
        at = pl.ds(p * strip, strip)
        copies.append(
            [
                pltpu.make_async_copy(src, dst.at[at], sems.at[p, n])
                for n, (src, dst) in enumerate(
                    (
                        (bits_hbm.at[0, at, cols], draws),
                        (inner_hbm.at[0, ids[0], at, cols], chosen),
                        (snap_hbm.at[at, cols], snaps),
                    )
                )
            ]
        )
        for c in copies[-1]:
            c.start()
    for p in range(PIECES):
        for c in copies[p]:
            c.wait()
        for k in range(Y):
            owner = lax.rem(here() + k, Y)
            for j in range(PER):
                for i in range(strip // 16):
                    at = pl.ds(p * strip + i * 16, 16)
                    block = pl.ds(pl.multiple_of((j * Y + owner) * share, share), share)
                    raw = snaps[at, block]
                    snap = grid_scale * raw.astype(jnp.float32)
                    kept = grid_scale * chosen[at, block].astype(jnp.float32)
                    level = draws[at, block].astype(jnp.float32) * (1.0 / bit_levels)
                    centred = jnp.ceil((snap - kept) - level) - jnp.floor(snap)
                    outs[k][at, j * share : (j + 1) * share] = centred.astype(jnp.bfloat16)
                    if k == 0:
                        snap_out[at, j * share : (j + 1) * share] = raw


def rounded_blocks(ids, after, inner, snapshot, bits, chunk, share):
    rows = snapshot.shape[0]
    wide = PER * Y * share
    return pl.pallas_call(
        functools.partial(round_kernel, chunk, share),
        out_shape=[pltpu.VMEM((rows, PER * share), jnp.bfloat16)] * (Y + 1)
        + [pltpu.VMEM((rows, wide), jnp.bfloat16)],
        in_specs=[pl.BlockSpec(memory_space=pltpu.SMEM)]
        + [pl.BlockSpec(memory_space=pl.ANY)]
        + [pl.BlockSpec(memory_space=pltpu.HBM)] * 3,
        out_specs=[pl.BlockSpec(memory_space=pltpu.VMEM)] * (Y + 2),
        scratch_shapes=[
            pltpu.VMEM((rows, wide), jnp.bfloat16),
            pltpu.VMEM((rows, wide), jnp.int32),
            pltpu.SemaphoreType.DMA((PIECES, 3)),
        ],
        compiler_params=pltpu.CompilerParams(vmem_limit_bytes=12 << 20),
        cost_estimate=pl.CostEstimate(
            flops=12 * rows * wide, bytes_accessed=10 * rows * wide, transcendentals=0
        ),
        name=f"round{chunk}",
    )(ids, after, pinned(inner), pinned(snapshot), pinned(bits))


def copy_kernel(ids, after_ref, inner_hbm, out_hbm, held, sems):
    frags = inner_hbm.shape[1]
    rows = inner_hbm.shape[2]
    strip = rows // PIECES
    steps = []
    for n in range(1, frags):
        f = lax.rem(ids[0] + n, frags)
        for p in range(PIECES):
            at = pl.ds(p * strip, strip)
            slot = held.at[n - 1, at]
            steps.append(
                (
                    pltpu.make_async_copy(inner_hbm.at[0, f, at], slot, sems.at[n - 1, p, 0]),
                    pltpu.make_async_copy(slot, out_hbm.at[0, f, at], sems.at[n - 1, p, 1]),
                )
            )
    for load, _ in steps:
        load.start()
    for load, store in steps:
        load.wait()
        store.start()
    for _, store in steps:
        store.wait()


def others_copied(ids, after, inner):
    frags = inner.shape[1]
    return pl.pallas_call(
        copy_kernel,
        out_shape=jax.ShapeDtypeStruct(inner.shape, inner.dtype),
        in_specs=[
            pl.BlockSpec(memory_space=pltpu.SMEM),
            pl.BlockSpec(memory_space=pl.ANY),
            pl.BlockSpec(memory_space=pltpu.HBM),
        ],
        out_specs=pl.BlockSpec(memory_space=pltpu.HBM),
        scratch_shapes=[
            pltpu.VMEM((frags - 1, *inner.shape[2:]), inner.dtype),
            pltpu.SemaphoreType.DMA((frags - 1, PIECES, 2)),
        ],
        compiler_params=pltpu.CompilerParams(vmem_limit_bytes=12 << 20),
        cost_estimate=pl.CostEstimate(flops=0, bytes_accessed=3 * inner.size, transcendentals=0),
        name="others",
    )(ids, after, pinned(inner))


def blend_kernel(chunk, share, ids, chosen, *refs):
    blocks = refs[:Y]
    snap_hbm, inner_out, snaps, mixed, sems = refs[-5:]
    rows = snaps.shape[0]
    wide = PER * Y * share
    strip = rows // PIECES
    cols = pl.ds(chunk * wide, wide)
    copies = []
    for p in range(PIECES):
        for n, k in enumerate(ORDER):
            owner = lax.rem(here() + Y - k, Y)
            for j in range(PER):
                for i in range(strip // 16):
                    at = pl.ds(p * strip + i * 16, 16)
                    block = pl.ds(pl.multiple_of((j * Y + owner) * share, share), share)
                    new = blocks[n][at, j * share : (j + 1) * share]
                    snaps[at, block] = new
                    mixed[at, block] = (
                        blend_keep * chosen[at, block].astype(jnp.float32)
                        + (1.0 - blend_keep) * new.astype(jnp.float32)
                    ).astype(jnp.bfloat16)
        at = pl.ds(p * strip, strip)
        copies += [
            pltpu.make_async_copy(snaps.at[at], snap_hbm.at[at, cols], sems.at[p, 0]),
            pltpu.make_async_copy(mixed.at[at], inner_out.at[0, ids[0], at, cols], sems.at[p, 1]),
        ]
        for c in copies[-2:]:
            c.start()
    for c in copies:
        c.wait()


def blended(ids, chosen, blocks, snap_out, inner_out, chunk, share):
    rows = blocks[0].shape[0]
    wide = PER * Y * share
    kept = [inner_out] if snap_out is None else [snap_out, inner_out]
    last = 1 + 1 + Y + len(kept) - 1
    aliases = {last: 1} if snap_out is None else {last - 1: 0, last: 1}
    hbm = pl.BlockSpec(memory_space=pltpu.HBM)
    return pl.pallas_call(
        functools.partial(blend_kernel, chunk, share),
        out_shape=[
            jax.ShapeDtypeStruct((rows, CHUNKS * wide), jnp.bfloat16),
            jax.ShapeDtypeStruct(inner_out.shape, inner_out.dtype),
        ],
        in_specs=[pl.BlockSpec(memory_space=pltpu.SMEM)]
        + [pl.BlockSpec(memory_space=pltpu.VMEM)] * (Y + 1)
        + [hbm] * len(kept),
        out_specs=[hbm, hbm],
        scratch_shapes=[pltpu.VMEM((rows, wide), jnp.bfloat16)] * 2
        + [pltpu.SemaphoreType.DMA((PIECES, 2))],
        input_output_aliases=aliases,
        compiler_params=pltpu.CompilerParams(vmem_limit_bytes=12 << 20),
        cost_estimate=pl.CostEstimate(
            flops=4 * rows * wide, bytes_accessed=8 * rows * wide, transcendentals=0
        ),
        name=f"blend{chunk}",
    )(ids, chosen, *blocks, *kept)


def body(inner, snapshot, momentum, bits, fragment):
    f32, bf16 = jnp.float32, jnp.bfloat16
    share = momentum.shape[1]
    me = lax.axis_index("replica")
    y, z = lax.rem(me, Y), lax.div(me, Y)
    ids = fragment

    def send(x, perm):
        return lax.ppermute(x, "replica", perm)

    near = send(momentum, z_swap(1))
    odd = lax.rem(z, 2) == 1
    mine = [jnp.where(odd, near, momentum), jnp.where(odd, momentum, near)]
    both = jnp.concatenate(mine, axis=1)
    far = send(both, z_swap(3))
    far = [far[:, :share], far[:, share:]]
    high = lax.div(z, 2) == 1
    moments = [jnp.where(high, b, a) for a, b in zip(mine, far)]
    moments += [jnp.where(high, a, b) for a, b in zip(mine, far)]

    sent, parts, snaps, kept = [], [], [], []
    for c in range(CHUNKS):
        *blocks, snap, chosen = rounded_blocks(
            ids, ids if c == 0 else both, inner, snapshot, bits, c, share
        )
        sent.append(blocks)
        snaps.append(snap)
        kept.append(chosen)
    for c in range(CHUNKS):
        got = [sent[c][0]] + [send(sent[c][k], y_shift(k)) for k in (1, 2, 3)]
        parts.append(sum(g.astype(f32) for g in got).astype(bf16))
    others = others_copied(ids, moments[0], inner)
    grads, news = [], []
    for c in range(CHUNKS):
        order = (1, 3) if c % 2 == 0 else (3, 1)
        part = parts[c]
        part = (part.astype(f32) + send(part, z_swap(order[0])).astype(f32)).astype(bf16)
        if c == CHUNKS - 1:
            part, others = lax.optimization_barrier((part, others))
        total = part.astype(f32) + send(part, z_swap(order[1])).astype(f32)
        snap = snaps[c].astype(f32)
        grad = (total + (Y * Z) * jnp.floor(grid_scale * snap)) / (grid_scale * Y * Z)
        gathered = jnp.concatenate([moments[c * PER + j] for j in range(PER)], axis=1)
        moment = momentum_coef * gathered + grad
        grads.append(grad)
        news.append((snap - outer_rate * (grad + momentum_coef * moment)).astype(bf16))

    snap_out, inner_out = None, others
    for c in range(CHUNKS):
        blocks = [news[c]] + [send(news[c], y_shift(k)) for k in ORDER[1:]]
        snap_out, inner_out = blended(ids, kept[c], blocks, snap_out, inner_out, c, share)

    own = grads[0][:, :share]
    for b in range(1, Z):
        at = (b % PER) * share
        own = jnp.where(z == b, grads[b // PER][:, at : at + share], own)
    return snap_out, momentum_coef * momentum + own, inner_out


def solution(mesh):
    placed = (
        P("replica", None, "fsdp", None),
        P("fsdp", None),
        P("fsdp", "replica"),
        P("replica", "fsdp", None),
        P(),
    )
    return jax.shard_map(
        body,
        mesh=mesh,
        in_specs=placed,
        out_specs=(P("fsdp", None), P("fsdp", "replica"), P("replica", None, "fsdp", None)),
        check_vma=False,
    )
```

```python
import functools

import jax
import jax.numpy as jnp
from jax import lax
from jax.experimental import pallas as pl
from jax.experimental.pallas import tpu as pltpu
from jax.sharding import PartitionSpec as P

momentum_coef = 0.9
outer_rate = 0.7
blend_keep = 0.5
grid_scale = 4.0
bit_levels = 4096.0

Y = 4
Z = 4
CHUNKS = 2
PER = Z // CHUNKS
PIECES = 2
ORDER = (0, 3, 1, 2)


def y_shift(k):
    return [(z * Y + y, z * Y + (y + k) % Y) for z in range(Z) for y in range(Y)]


def z_swap(s):
    return [(z * Y + y, (z ^ s) * Y + y) for z in range(Z) for y in range(Y)]


def here():
    return lax.rem(lax.axis_index("replica"), Y)


def pinned(x):
    return pltpu.with_memory_space_constraint(x, pltpu.HBM)


def round_kernel(chunk, share, ids, after_ref, inner_hbm, snap_hbm, bits_hbm, *refs):
    outs, snap_out, chosen = refs[:Y], refs[Y], refs[Y + 1]
    snaps, draws, sems = refs[Y + 2 :]
    rows = snaps.shape[0]
    wide = PER * Y * share
    strip = rows // PIECES
    cols = pl.ds(chunk * wide, wide)
    copies = []
    for p in range(PIECES):
        at = pl.ds(p * strip, strip)
        copies.append(
            [
                pltpu.make_async_copy(src, dst.at[at], sems.at[p, n])
                for n, (src, dst) in enumerate(
                    (
                        (bits_hbm.at[0, at, cols], draws),
                        (inner_hbm.at[0, ids[0], at, cols], chosen),
                        (snap_hbm.at[at, cols], snaps),
                    )
                )
            ]
        )
        for c in copies[-1]:
            c.start()
    for p in range(PIECES):
        for c in copies[p]:
            c.wait()
        for k in range(Y):
            owner = lax.rem(here() + k, Y)
            for j in range(PER):
                for i in range(strip // 16):
                    at = pl.ds(p * strip + i * 16, 16)
                    block = pl.ds(pl.multiple_of((j * Y + owner) * share, share), share)
                    raw = snaps[at, block]
                    snap = grid_scale * raw.astype(jnp.float32)
                    kept = grid_scale * chosen[at, block].astype(jnp.float32)
                    level = draws[at, block].astype(jnp.float32) * (1.0 / bit_levels)
                    centred = jnp.ceil((snap - kept) - level) - jnp.floor(snap)
                    outs[k][at, j * share : (j + 1) * share] = centred.astype(jnp.bfloat16)
                    if k == 0:
                        snap_out[at, j * share : (j + 1) * share] = raw


def rounded_blocks(ids, after, inner, snapshot, bits, chunk, share):
    rows = snapshot.shape[0]
    wide = PER * Y * share
    return pl.pallas_call(
        functools.partial(round_kernel, chunk, share),
        out_shape=[pltpu.VMEM((rows, PER * share), jnp.bfloat16)] * (Y + 1)
        + [pltpu.VMEM((rows, wide), jnp.bfloat16)],
        in_specs=[pl.BlockSpec(memory_space=pltpu.SMEM)]
        + [pl.BlockSpec(memory_space=pl.ANY)]
        + [pl.BlockSpec(memory_space=pltpu.HBM)] * 3,
        out_specs=[pl.BlockSpec(memory_space=pltpu.VMEM)] * (Y + 2),
        scratch_shapes=[
            pltpu.VMEM((rows, wide), jnp.bfloat16),
            pltpu.VMEM((rows, wide), jnp.int32),
            pltpu.SemaphoreType.DMA((PIECES, 3)),
        ],
        compiler_params=pltpu.CompilerParams(vmem_limit_bytes=12 << 20),
        cost_estimate=pl.CostEstimate(
            flops=12 * rows * wide, bytes_accessed=10 * rows * wide, transcendentals=0
        ),
        name=f"round{chunk}",
    )(ids, after, pinned(inner), pinned(snapshot), pinned(bits))


def copy_kernel(ids, after_ref, inner_hbm, out_hbm, held, sems):
    frags = inner_hbm.shape[1]
    rows = inner_hbm.shape[2]
    strip = rows // PIECES
    steps = []
    for n in range(1, frags):
        f = lax.rem(ids[0] + n, frags)
        for p in range(PIECES):
            at = pl.ds(p * strip, strip)
            slot = held.at[n - 1, at]
            steps.append(
                (
                    pltpu.make_async_copy(inner_hbm.at[0, f, at], slot, sems.at[n - 1, p, 0]),
                    pltpu.make_async_copy(slot, out_hbm.at[0, f, at], sems.at[n - 1, p, 1]),
                )
            )
    for load, _ in steps:
        load.start()
    for load, store in steps:
        load.wait()
        store.start()
    for _, store in steps:
        store.wait()


def others_copied(ids, after, inner):
    frags = inner.shape[1]
    return pl.pallas_call(
        copy_kernel,
        out_shape=jax.ShapeDtypeStruct(inner.shape, inner.dtype),
        in_specs=[
            pl.BlockSpec(memory_space=pltpu.SMEM),
            pl.BlockSpec(memory_space=pl.ANY),
            pl.BlockSpec(memory_space=pltpu.HBM),
        ],
        out_specs=pl.BlockSpec(memory_space=pltpu.HBM),
        scratch_shapes=[
            pltpu.VMEM((frags - 1, *inner.shape[2:]), inner.dtype),
            pltpu.SemaphoreType.DMA((frags - 1, PIECES, 2)),
        ],
        compiler_params=pltpu.CompilerParams(vmem_limit_bytes=12 << 20),
        cost_estimate=pl.CostEstimate(flops=0, bytes_accessed=3 * inner.size, transcendentals=0),
        name="others",
    )(ids, after, pinned(inner))


def blend_kernel(chunk, share, ids, chosen, *refs):
    blocks = refs[:Y]
    snap_hbm, inner_out, snaps, mixed, sems = refs[-5:]
    rows = snaps.shape[0]
    wide = PER * Y * share
    strip = rows // PIECES
    cols = pl.ds(chunk * wide, wide)
    copies = []
    for p in range(PIECES):
        for n, k in enumerate(ORDER):
            owner = lax.rem(here() + Y - k, Y)
            for j in range(PER):
                for i in range(strip // 16):
                    at = pl.ds(p * strip + i * 16, 16)
                    block = pl.ds(pl.multiple_of((j * Y + owner) * share, share), share)
                    new = blocks[n][at, j * share : (j + 1) * share]
                    snaps[at, block] = new
                    mixed[at, block] = (
                        blend_keep * chosen[at, block].astype(jnp.float32)
                        + (1.0 - blend_keep) * new.astype(jnp.float32)
                    ).astype(jnp.bfloat16)
        at = pl.ds(p * strip, strip)
        copies += [
            pltpu.make_async_copy(snaps.at[at], snap_hbm.at[at, cols], sems.at[p, 0]),
            pltpu.make_async_copy(mixed.at[at], inner_out.at[0, ids[0], at, cols], sems.at[p, 1]),
        ]
        for c in copies[-2:]:
            c.start()
    for c in copies:
        c.wait()


def blended(ids, chosen, blocks, snap_out, inner_out, chunk, share):
    rows = blocks[0].shape[0]
    wide = PER * Y * share
    kept = [inner_out] if snap_out is None else [snap_out, inner_out]
    last = 1 + 1 + Y + len(kept) - 1
    aliases = {last: 1} if snap_out is None else {last - 1: 0, last: 1}
    hbm = pl.BlockSpec(memory_space=pltpu.HBM)
    return pl.pallas_call(
        functools.partial(blend_kernel, chunk, share),
        out_shape=[
            jax.ShapeDtypeStruct((rows, CHUNKS * wide), jnp.bfloat16),
            jax.ShapeDtypeStruct(inner_out.shape, inner_out.dtype),
        ],
        in_specs=[pl.BlockSpec(memory_space=pltpu.SMEM)]
        + [pl.BlockSpec(memory_space=pltpu.VMEM)] * (Y + 1)
        + [hbm] * len(kept),
        out_specs=[hbm, hbm],
        scratch_shapes=[pltpu.VMEM((rows, wide), jnp.bfloat16)] * 2
        + [pltpu.SemaphoreType.DMA((PIECES, 2))],
        input_output_aliases=aliases,
        compiler_params=pltpu.CompilerParams(vmem_limit_bytes=12 << 20),
        cost_estimate=pl.CostEstimate(
            flops=4 * rows * wide, bytes_accessed=8 * rows * wide, transcendentals=0
        ),
        name=f"blend{chunk}",
    )(ids, chosen, *blocks, *kept)


def body(inner, snapshot, momentum, bits, fragment):
    f32, bf16 = jnp.float32, jnp.bfloat16
    share = momentum.shape[1]
    me = lax.axis_index("replica")
    y, z = lax.rem(me, Y), lax.div(me, Y)
    ids = fragment

    def send(x, perm):
        return lax.ppermute(x, "replica", perm)

    near = send(momentum, z_swap(1))
    odd = lax.rem(z, 2) == 1
    mine = [jnp.where(odd, near, momentum), jnp.where(odd, momentum, near)]
    both = jnp.concatenate(mine, axis=1)
    far = send(both, z_swap(3))
    far = [far[:, :share], far[:, share:]]
    high = lax.div(z, 2) == 1
    moments = [jnp.where(high, b, a) for a, b in zip(mine, far)]
    moments += [jnp.where(high, a, b) for a, b in zip(mine, far)]

    sent, parts, snaps, kept = [], [], [], []
    for c in range(CHUNKS):
        *blocks, snap, chosen = rounded_blocks(
            ids, ids if c == 0 else both, inner, snapshot, bits, c, share
        )
        sent.append(blocks)
        snaps.append(snap)
        kept.append(chosen)
    for c in range(CHUNKS):
        got = [sent[c][0]] + [send(sent[c][k], y_shift(k)) for k in (1, 2, 3)]
        parts.append(sum(g.astype(f32) for g in got).astype(bf16))
    others = others_copied(ids, moments[0], inner)
    grads, news = [], []
    for c in range(CHUNKS):
        order = (1, 3)
        part = parts[c]
        part = (part.astype(f32) + send(part, z_swap(order[0])).astype(f32)).astype(bf16)
        if c == CHUNKS - 1:
            part, others = lax.optimization_barrier((part, others))
        total = part.astype(f32) + send(part, z_swap(order[1])).astype(f32)
        snap = snaps[c].astype(f32)
        grad = (total + (Y * Z) * jnp.floor(grid_scale * snap)) / (grid_scale * Y * Z)
        gathered = jnp.concatenate([moments[c * PER + j] for j in range(PER)], axis=1)
        moment = momentum_coef * gathered + grad
        grads.append(grad)
        news.append((snap - outer_rate * (grad + momentum_coef * moment)).astype(bf16))

    snap_out, inner_out = None, others
    for c in range(CHUNKS):
        blocks = [news[c]] + [send(news[c], y_shift(k)) for k in ORDER[1:]]
        snap_out, inner_out = blended(ids, kept[c], blocks, snap_out, inner_out, c, share)

    own = grads[0][:, :share]
    for b in range(1, Z):
        at = (b % PER) * share
        own = jnp.where(z == b, grads[b // PER][:, at : at + share], own)
    return snap_out, momentum_coef * momentum + own, inner_out


def solution(mesh):
    placed = (
        P("replica", None, "fsdp", None),
        P("fsdp", None),
        P("fsdp", "replica"),
        P("replica", "fsdp", None),
        P(),
    )
    return jax.shard_map(
        body,
        mesh=mesh,
        in_specs=placed,
        out_specs=(P("fsdp", None), P("fsdp", "replica"), P("replica", None, "fsdp", None)),
        check_vma=False,
    )
```
